32 devices in a mesh: grp: 4 (over y, x), ep: 8 (over z, core).
Axes of the slice: x: 2, y: 2, z: 4, core: 2. Of those that a mesh axis runs over, the one named last changes fastest.
Arguments:
- tokens: bfloat16 [4096, 2048], P(('grp', 'ep')), may hold values from -6 to 6
- routes: int32 [4096, 6], P(('grp', 'ep')), may hold values from 0 to 7, all different within a row; in each aligned block of 128 rows (0 to 127, 128 to 255, ...) at most 128 rows name the same one
- route_gain: float32 [4096, 6], P(('grp', 'ep')), may hold values from 0.05 to 0.6
- gate_weight: bfloat16 [8, 2048, 768], P('ep', 'grp'), may hold values from -0.125 to 0.125
- up_weight: bfloat16 [8, 2048, 768], P('ep', 'grp'), may hold values from -0.125 to 0.125
- down_weight: bfloat16 [8, 768, 2048], P('ep', None, 'grp'), may hold values from -0.21875 to 0.21875
- norm_gain: float32 [2048], replicated, may hold values from 0.25 to 1.75
- query_weight: bfloat16 [2048, 1536], P(None, 'grp'), may hold values from -0.125 to 0.125
Outputs:
- mixed: bfloat16 [4096, 2048], P(('grp', 'ep'))
- query: bfloat16 [4096, 1536], P(('grp', 'ep'))
The draws below stay inside these ranges and needn't reach their ends.
Inputs may be any that keep to these rules, and one draw needn't show every extreme that they name: `routes`: each row names 6 different experts. Among the 128 rows of one device no expert is named by more than 128 rows, a bound that some of them reach.
All inputs are finite; a program needn't handle non-finite values.
Results may differ from the reference program's by a relative error of at most 0.0053.
Values may be sent and summed in bfloat16 or wider, within the bound.
A program may use at most 128 MiB of HBM per device.

```python
import math
import jax
import jax.numpy as jnp
import numpy as np
from jax import lax

D = 2048
FF_E = 768
QW = 1536
TOP = 6
TOK_DEV = 128
EXPERTS = 8
CAP = 128
TOKENS = 4096
N_GRP = 4
N_EP = 8


def block_levels(rng, shape, shards, smallest, largest):
    factor_of, own = 1.0, jax.random.fold_in(rng, 6)
    for axis_at, shards_of in shards:
        draws = jnp.exp(jax.random.uniform(jax.random.fold_in(own, axis_at), (shards_of,), jnp.float32, smallest / len(shards), largest / len(shards)))
        factor_of = factor_of * jnp.repeat(draws, shape[axis_at] // shards_of).reshape([-1 if axis == axis_at else 1 for axis in range(len(shape))])
    return factor_of


def routed_block(rng, own, number, rows, amount, top, limit, lean):
    ranking = jax.random.permutation(rng, amount)
    packed, ordinary = load_shares(amount, rows * top, limit, lean, True), load_shares(amount, rows * top, limit, lean, False)
    places = jnp.arange(amount)

    def named(tallies, offset_by):
        used = int((tallies > 0).sum())
        fixed = max(1, used // 4)
        passed = fixed + (places - fixed + offset_by * (used - fixed)) % max(1, amount - fixed)
        return jnp.zeros((amount,), jnp.int32).at[ranking[jnp.where(places < fixed, places, passed)]].set(jnp.asarray(tallies, jnp.int32))

    tallies = jnp.where(number % 4 == 0, named(packed, number // 4), named(ordinary, number - number // 4 - 1))
    mixed = jax.random.permutation(jax.random.fold_in(own, 3), amount)
    source_of, sink = mixed[0:amount // 2 * 2:2], mixed[1:amount // 2 * 2:2]
    margin = jnp.minimum(tallies[source_of] - 1, limit - tallies[sink]) // 2
    margin = jnp.where((source_of == ranking[0]) | (sink == ranking[0]) | (tallies[sink] == 0), 0, jnp.maximum(margin, 0))
    passed = jax.random.randint(jax.random.fold_in(own, 4), (amount // 2,), 0, 1 << 20) % (margin + 1)
    tallies = tallies.at[source_of].add(-passed).at[sink].add(passed)
    items = jnp.searchsorted(jnp.cumsum(tallies), jnp.arange(rows * top), side="right").astype(jnp.int32)
    listing = items.reshape(top, rows).T
    listing = listing[jax.random.permutation(jax.random.fold_in(own, 1), rows)]
    offset_by = jax.random.randint(jax.random.fold_in(own, 2), (rows, 1), 0, top)
    return jnp.take_along_axis(listing, (jnp.arange(top)[None, :] + offset_by) % top, axis=1)


def load_shares(number_of, total, most, slope, full):
    loads = [(1 << 20) // math.isqrt(grade ** slope) + 1 for grade in range(1, number_of + 1)]
    largest = most if full else min(most, max(-(-total // number_of), total * loads[0] // sum(loads)))
    least = 1 if total - largest >= number_of - 1 else 0
    counts, spare = [largest] + [least] * (number_of - 1), total - largest - least * (number_of - 1)
    while spare > 0:
        free = [i for i in range(1, number_of) if counts[i] < largest] or [i for i in range(1, number_of) if counts[i] < most]
        mass, budget = sum([loads[i] for i in free]), spare
        for i in free:
            addition = min(most - counts[i], max(1, budget * loads[i] // mass), spare)
            counts[i] = counts[i] + addition
            spare = spare - addition
    return np.array(counts)


def bell_draw(stream_key, dims, scale, reach, split=(), held_as=jnp.bfloat16):
    entries = scale * jax.random.normal(stream_key, dims, jnp.float32)
    if split:
        entries = entries * block_levels(stream_key, dims, split, -0.22, 0.18)
    return jnp.clip(entries, -reach, reach).astype(held_as)


def setup_inputs(seed: int = 0) -> dict:
    key_of = jax.random.split(jax.random.key(seed), 9)
    tokens = bell_draw(key_of[0], (TOKENS, D), 1.0, 6.0, ((0, 32),))
    routes_keys = jax.random.split(jax.random.fold_in(key_of[1], 1), TOKENS // TOK_DEV)
    routes_turns = jax.random.permutation(jax.random.fold_in(key_of[1], 3), TOKENS // TOK_DEV)
    routes = jax.vmap(lambda own, number: routed_block(jax.random.fold_in(key_of[1], 2), own, number, TOK_DEV, EXPERTS, TOP, CAP, 2))(routes_keys, routes_turns).reshape((TOKENS, TOP))
    route_gain = jnp.clip(jnp.exp(math.log(0.6) - 2.4849067 * jax.random.uniform(key_of[2], (TOKENS, TOP), jnp.float32) ** block_levels(key_of[2], (TOKENS, TOP), ((0, 32),), -0.2, 0.2)), 0.05, 0.6)
    gate_weight = bell_draw(key_of[3], (EXPERTS, D, FF_E), D ** -0.5, 0.125, ((0, 8), (1, 4)))
    up_weight = bell_draw(key_of[4], (EXPERTS, D, FF_E), D ** -0.5, 0.125, ((0, 8), (1, 4)))
    down_weight = bell_draw(key_of[5], (EXPERTS, FF_E, D), FF_E ** -0.5, 0.21875, ((0, 8), (2, 4)))
    norm_gain = jnp.clip(1.0 + 0.15 * jax.random.normal(key_of[6], (D,), jnp.float32), 0.25, 1.75)
    query_weight = bell_draw(key_of[7], (D, QW), D ** -0.5, 0.125, ((1, 4),))
    return dict(tokens=tokens, routes=routes, route_gain=route_gain, gate_weight=gate_weight, up_weight=up_weight, down_weight=down_weight, norm_gain=norm_gain, query_weight=query_weight)


def expert_apply(rows, wg, wu, wd):
    gate = jnp.dot(rows, wg, preferred_element_type=jnp.float32)
    up = jnp.dot(rows, wu, preferred_element_type=jnp.float32)
    hidden = (jax.nn.silu(gate) * up).astype(jnp.bfloat16)
    return jnp.dot(hidden, wd, preferred_element_type=jnp.float32).astype(jnp.bfloat16)

def reference(tokens, routes, route_gain, gate_weight, up_weight, down_weight, norm_gain, query_weight):
    flat = routes.reshape(-1)
    weight_flat = route_gain.reshape(-1)
    bucket = N_GRP * N_EP * CAP

    def one_expert(acc, expert):
        chosen = flat == expert
        index = jnp.nonzero(chosen, size=bucket, fill_value=0)[0]
        live = (jnp.arange(bucket) < jnp.sum(chosen)).astype(jnp.float32)
        source = index // TOP
        rows = tokens[source]
        answer = expert_apply(rows, gate_weight[expert], up_weight[expert], down_weight[expert]).astype(jnp.float32)
        acc = acc.at[source].add(answer * (weight_flat[index] * live)[:, None])
        return (acc, None)
    acc, _ = lax.scan(one_expert, jnp.zeros((TOKENS, D), jnp.float32), jnp.arange(EXPERTS))
    total = tokens.astype(jnp.float32) + acc
    square = lax.optimization_barrier(jnp.mean(total * total, axis=-1, keepdims=True))
    normed = (total * lax.rsqrt(square + 1e-06) * norm_gain).astype(jnp.bfloat16)
    query = jnp.dot(normed, query_weight, preferred_element_type=jnp.float32).astype(jnp.bfloat16)
    return (total.astype(jnp.bfloat16), query)
```

```python
import jax
import jax.numpy as jnp
from jax import lax
from jax.sharding import PartitionSpec as P


def shards(
    tokens, routes, route_gain, gate_weight, up_weight, down_weight, norm_gain, query_weight
):
    ep = lax.axis_index("ep")
    rows = lax.all_gather(tokens, "ep", axis=0, tiled=True)
    named = lax.all_gather(routes, "ep", axis=0, tiled=True)
    gains = lax.all_gather(route_gain, "ep", axis=0, tiled=True)
    scale = jnp.sum(jnp.where(named == ep, gains, 0.0), axis=1, keepdims=True)
    gate = jnp.dot(
        rows,
        lax.all_gather(gate_weight[0], "grp", axis=0, tiled=True),
        preferred_element_type=jnp.float32,
    )
    up = jnp.dot(
        rows,
        lax.all_gather(up_weight[0], "grp", axis=0, tiled=True),
        preferred_element_type=jnp.float32,
    )
    hidden = (jax.nn.silu(gate) * up).astype(jnp.bfloat16)
    answers = jnp.dot(
        hidden,
        lax.all_gather(down_weight[0], "grp", axis=1, tiled=True),
        preferred_element_type=jnp.float32,
    )
    answers = (answers * scale).astype(jnp.bfloat16)
    summed = lax.psum_scatter(answers, "ep", scatter_dimension=0, tiled=True)
    total = tokens.astype(jnp.float32) + summed.astype(jnp.float32)
    square = jnp.mean(total * total, axis=-1, keepdims=True)
    normed = (total * lax.rsqrt(square + 1e-06) * norm_gain).astype(jnp.bfloat16)
    query = jnp.dot(
        normed,
        lax.all_gather(query_weight, "grp", axis=1, tiled=True),
        preferred_element_type=jnp.float32,
    ).astype(jnp.bfloat16)
    return (total.astype(jnp.bfloat16), query)


def solution(mesh):
    placed = (
        P(("grp", "ep"), None),
        P(("grp", "ep"), None),
        P(("grp", "ep"), None),
        P("ep", "grp", None),
        P("ep", "grp", None),
        P("ep", None, "grp"),
        P(),
        P(None, "grp"),
    )
    return jax.shard_map(
        shards,
        mesh=mesh,
        in_specs=placed,
        out_specs=(P(("grp", "ep"), None), P(("grp", "ep"), None)),
        check_vma=False,
    )
```

```python
import jax
import jax.numpy as jnp
from jax import lax
from jax.experimental import pallas as pl
from jax.experimental.pallas import tpu as pltpu
from jax.sharding import PartitionSpec as P

MESH = pl.DeviceIdType.MESH
NZ = 4


def kernel(
    tok, gtab, gw, uw, dw, ng, qw, mixed, query,
    rows, gains, scale, gin, uin, din, qin, acc_g, acc_u, hid,
    sout, sin, part, rin, lin, rout, total, normed,
    gain_s, gain_r, tok_r, tok_sr, tok_sl, tok_ss, w_s, w_r, q_s, q_r,
    sib_s, sib_r, right_s, right_r, left_s, left_r,
):
    g = lax.axis_index("grp")
    ep = lax.axis_index("ep")
    z = ep // 2
    c = ep % 2
    gx = g + 1 - 2 * (g % 2)
    gy = (g + 2) % 4
    gd = 3 - g
    x_dev, y_dev = (gx, ep), (gy, ep)
    sib = (g, ep + 1 - 2 * c)
    nxt, prv = (g, ep + 2), (g, ep - 2)
    n_tok, width = tok.shape
    depth = gw.shape[0]
    cols = dw.shape[1]
    qcols = qw.shape[1]
    has_next, has_prev = z < NZ - 1, z > 0

    def remote(src, dst, s, r, dev):
        return pltpu.make_async_remote_copy(
            src_ref=src, dst_ref=dst, send_sem=s, recv_sem=r, device_id=dev, device_id_type=MESH
        )

    barrier = pltpu.get_barrier_semaphore()
    for k in range(1, 2 * NZ):
        pl.semaphore_signal(barrier, inc=1, device_id=(g, (ep + k) % (2 * NZ)), device_id_type=MESH)
    for dev in (x_dev, y_dev):
        pl.semaphore_signal(barrier, inc=1, device_id=dev, device_id_type=MESH)
    pl.semaphore_wait(barrier, 2 * NZ + 1)

    def block(zz, cc):
        return rows.at[pl.ds(pl.multiple_of((cc * NZ + zz) * n_tok, n_tok), n_tok)]

    def tok_copy(src, zz, send, dev):
        return remote(src, block(zz, c), send.at[zz], tok_r.at[c * NZ + zz], dev)

    def tok_wait(zz, cc):
        ref = block(zz, cc)
        remote(ref, ref, tok_ss.at[0], tok_r.at[cc * NZ + zz], sib).wait_recv()

    @pl.when(has_next)
    def _():
        tok_copy(tok, z, tok_sr, nxt).start()

    @pl.when(has_prev)
    def _():
        tok_copy(tok, z, tok_sl, prv).start()

    tok_copy(tok, z, tok_ss, sib).start()

    shards_of = ((gw, gin), (uw, uin), (dw, din))

    def own_x(i):
        src, dst = shards_of[i]
        return remote(src, dst.at[0], w_s.at[i, 0], w_r.at[i, 0], x_dev)

    def own_y(i):
        src, dst = shards_of[i]
        return remote(src, dst.at[1], w_s.at[i, 1], w_r.at[i, 1], y_dev)

    def relay_y(i):
        dst = shards_of[i][1]
        half = dst.shape[1] // 2
        return remote(
            dst.at[0, pl.ds(0, half)], dst.at[2, pl.ds(0, half)], w_s.at[i, 2], w_r.at[i, 2], y_dev
        )

    def relay_x(i):
        dst = shards_of[i][1]
        half = dst.shape[1] // 2
        return remote(
            dst.at[1, pl.ds(half, half)], dst.at[2, pl.ds(half, half)],
            w_s.at[i, 3], w_r.at[i, 3], x_dev,
        )

    own_x(0).start()
    own_y(0).start()
    own_x(1).start()
    own_y(1).start()

    def gain_copy(k):
        return remote(
            gtab, gains.at[c * NZ + z], gain_s.at[k], gain_r.at[c * NZ + z],
            (g, (ep + k) % (2 * NZ)),
        )

    for k in range(1, 2 * NZ):
        gain_copy(k).start()

    rows[pl.ds(pl.multiple_of((c * NZ + z) * n_tok, n_tok), n_tok), :] = tok[...]
    gains[c * NZ + z] = gtab[...]

    def hop(h):
        left, right = z - 1 - h, z + 1 + h

        @pl.when(left >= 0)
        def _():
            tok_wait(left, c)

            @pl.when(has_next)
            def _():
                tok_copy(block(left, c), left, tok_sr, nxt).start()

            tok_copy(block(left, c), left, tok_ss, sib).start()

        @pl.when(right <= NZ - 1)
        def _():
            tok_wait(right, c)

            @pl.when(has_prev)
            def _():
                tok_copy(block(right, c), right, tok_sl, prv).start()

            tok_copy(block(right, c), right, tok_ss, sib).start()

    def pass_on(i):
        own_x(i).wait_recv()
        relay_y(i).start()
        own_y(i).wait_recv()
        relay_x(i).start()

    hop(0)
    hop(1)
    pass_on(0)
    hop(2)
    pass_on(1)

    for k in range(1, 2 * NZ):
        peer = (ep + k) % (2 * NZ)
        at = (peer % 2) * NZ + peer // 2
        remote(gtab, gains.at[at], gain_s.at[0], gain_r.at[at], sib).wait_recv()
    for b in range(2 * NZ):
        table = gains[b]
        chosen = lax.broadcasted_iota(jnp.int32, table.shape, 0) == ep
        line = jnp.sum(jnp.where(chosen, table, 0.0), axis=0, keepdims=True)
        scale[b * n_tok : (b + 1) * n_tok, :] = jnp.broadcast_to(line, (n_tok, n_tok)).T
    for zz in range(NZ):
        tok_wait(zz, 1 - c)

    tile = 2 * n_tok
    tiles = rows.shape[0] // tile

    def partial(acc, w, owner, first):
        at = pl.ds(pl.multiple_of(owner * depth, depth), depth)

        def body(i, carry):
            r = pl.ds(pl.multiple_of(i * tile, tile), tile)
            p = jnp.dot(rows[r, at], w[...], preferred_element_type=jnp.float32)
            acc[r, :] = p if first else acc[r, :] + p
            return carry

        lax.fori_loop(0, tiles, body, 0)

    partial(acc_g, gw, g, True)
    partial(acc_u, uw, g, True)
    partial(acc_g, gin.at[0], gx, False)
    partial(acc_g, gin.at[1], gy, False)
    partial(acc_u, uin.at[0], gx, False)
    partial(acc_u, uin.at[1], gy, False)
    relay_y(0).wait_recv()
    relay_x(0).wait_recv()
    own_x(2).start()
    own_y(2).start()
    partial(acc_g, gin.at[2], gd, False)
    relay_y(1).wait_recv()
    relay_x(1).wait_recv()
    partial(acc_u, uin.at[2], gd, False)

    def act(i, carry):
        r = pl.ds(pl.multiple_of(i * n_tok, n_tok), n_tok)
        gate = acc_g[r, :]
        hid[r, :] = (gate / (1.0 + jnp.exp(-gate)) * acc_u[r, :]).astype(hid.dtype)
        return carry

    lax.fori_loop(0, rows.shape[0] // n_tok, act, 0)

    def sib_copy(q):
        return remote(sout.at[q], sin.at[q], sib_s.at[q], sib_r.at[q], sib)

    def answers(q, w):
        per = tile // n_tok

        def weighted(cc, i):
            at = pl.multiple_of(cc * NZ * n_tok + i * tile, tile)
            p = jnp.dot(hid[pl.ds(at, tile), :], w[...], preferred_element_type=jnp.float32)
            s = scale[pl.ds(at, tile), :]
            p = p * jnp.concatenate([s] * (cols // n_tok), axis=1)
            return p.reshape(per, n_tok, cols)

        def away(i, carry):
            sout[q, pl.ds(i * per, per)] = weighted(1 - c, i).astype(sout.dtype)
            return carry

        def here(i, carry):
            part[q, pl.ds(i * per, per)] = weighted(c, i)
            return carry

        lax.fori_loop(0, NZ // per, away, 0)
        sib_copy(q).start()
        lax.fori_loop(0, NZ // per, here, 0)
        sib_copy(q).wait_recv()

    def right_copy(q, d):
        return remote(rout.at[q, d], rin.at[q, d], right_s.at[q, d], right_r.at[q, d], nxt)

    def left_copy(q, d):
        return remote(rout.at[q, d], lin.at[q, d], left_s.at[q, d], left_r.at[q, d], prv)

    def ends(q):
        @pl.when(z == 0)
        def _():
            for d in range(NZ - 1, 0, -1):
                rout[q, d] = (part[q, d] + sin[q, d].astype(jnp.float32)).astype(rout.dtype)
                right_copy(q, d).start()

        @pl.when(z == NZ - 1)
        def _():
            for d in range(NZ - 1):
                rout[q, d] = (part[q, d] + sin[q, d].astype(jnp.float32)).astype(rout.dtype)
                left_copy(q, d).start()

    def chain(q, owner):
        for k in range(NZ - 1):
            d = NZ - 1 - k

            @pl.when((z > 0) & (z < d))
            def _():
                right_copy(q, d).wait_recv()
                rout[q, d] = (
                    part[q, d] + sin[q, d].astype(jnp.float32) + rin[q, d].astype(jnp.float32)
                ).astype(rout.dtype)
                right_copy(q, d).start()

            @pl.when((z < NZ - 1) & (z > k))
            def _():
                left_copy(q, k).wait_recv()
                rout[q, k] = (
                    part[q, k] + sin[q, k].astype(jnp.float32) + lin[q, k].astype(jnp.float32)
                ).astype(rout.dtype)
                left_copy(q, k).start()

        at = pl.ds(pl.multiple_of(owner * cols, cols), cols)
        total[:, at] = tok[:, at].astype(jnp.float32) + part[q, z] + sin[q, z].astype(jnp.float32)

        @pl.when(has_prev)
        def _():
            right_copy(q, z).wait_recv()
            total[:, at] = total[:, at] + rin[q, z].astype(jnp.float32)

        @pl.when(has_next)
        def _():
            left_copy(q, z).wait_recv()
            total[:, at] = total[:, at] + lin[q, z].astype(jnp.float32)

    q_half = qw.shape[0] // 2
    q_quarter = q_half // 2
    half_at = pl.ds(pl.multiple_of(c * q_half, q_half), q_half)
    first_at = pl.ds(pl.multiple_of(c * q_half, q_quarter), q_quarter)
    second_at = pl.ds(pl.multiple_of(c * q_half + q_quarter, q_quarter), q_quarter)

    def q_copy(k):
        if k == 0:
            return remote(qw.at[half_at], qin.at[0, half_at], q_s.at[0], q_r.at[0], x_dev)
        if k == 1:
            return remote(qw.at[half_at], qin.at[1, half_at], q_s.at[1], q_r.at[1], y_dev)
        if k == 2:
            return remote(qin.at[0, first_at], qin.at[2, first_at], q_s.at[2], q_r.at[2], y_dev)
        if k == 3:
            return remote(qin.at[1, second_at], qin.at[2, second_at], q_s.at[3], q_r.at[3], x_dev)
        slot, at = ((0, half_at), (1, half_at), (2, first_at), (2, second_at))[k - 4]
        return remote(qin.at[slot, at], qin.at[slot, at], q_s.at[k], q_r.at[k], sib)

    other_half = pl.ds(pl.multiple_of((1 - c) * q_half, q_half), q_half)
    other_first = pl.ds(pl.multiple_of((1 - c) * q_half, q_quarter), q_quarter)
    other_second = pl.ds(pl.multiple_of((1 - c) * q_half + q_quarter, q_quarter), q_quarter)

    def q_wait_sib(k):
        slot, at = ((0, other_half), (1, other_half), (2, other_first), (2, other_second))[k - 4]
        remote(qin.at[slot, at], qin.at[slot, at], q_s.at[k], q_r.at[k], sib).wait_recv()

    answers(0, dw)
    ends(0)
    chain(0, g)
    pass_on(2)
    answers(1, din.at[0])
    ends(1)
    answers(2, din.at[1])
    ends(2)
    relay_y(2).wait_recv()
    relay_x(2).wait_recv()
    q_copy(0).start()
    q_copy(1).start()
    chain(1, gx)
    answers(3, din.at[2])
    ends(3)
    chain(2, gy)
    q_copy(0).wait_recv()
    q_copy(2).start()
    q_copy(4).start()
    q_copy(1).wait_recv()
    q_copy(3).start()
    q_copy(5).start()
    chain(3, gd)

    value = total[...]
    mixed[...] = value.astype(mixed.dtype)
    square = jnp.sum(value * value, axis=-1, keepdims=True) * (1.0 / width)
    normed[...] = (value * lax.rsqrt(square + 1e-06) * ng[...]).astype(normed.dtype)

    def project(w, owner):
        at = pl.ds(pl.multiple_of(owner * qcols, qcols), qcols)
        query[:, at] = jnp.dot(
            normed[...], w[...], preferred_element_type=jnp.float32
        ).astype(query.dtype)

    project(qw, g)
    q_wait_sib(4)
    project(qin.at[0], gx)
    q_wait_sib(5)
    project(qin.at[1], gy)
    q_copy(2).wait_recv()
    q_copy(6).start()
    q_copy(3).wait_recv()
    q_copy(7).start()
    q_wait_sib(6)
    q_wait_sib(7)
    project(qin.at[2], gd)

    for k in range(1, 2 * NZ):
        gain_copy(k).wait_send()
    for zz in range(NZ):
        @pl.when(has_next & (zz <= z))
        def _():
            tok_copy(tok, zz, tok_sr, nxt).wait_send()

        @pl.when(has_prev & (zz >= z))
        def _():
            tok_copy(tok, zz, tok_sl, prv).wait_send()

        tok_copy(tok, zz, tok_ss, sib).wait_send()
    for i in range(3):
        for copy in (own_x, own_y, relay_x, relay_y):
            copy(i).wait_send()
    for k in range(8):
        q_copy(k).wait_send()
    for q in range(4):
        sib_copy(q).wait_send()
        for d in range(NZ):
            if d > 0:
                @pl.when(z < d)
                def _():
                    right_copy(q, d).wait_send()
            if d < NZ - 1:
                @pl.when(z > d)
                def _():
                    left_copy(q, d).wait_send()


def fused(tokens, routes, route_gain, gate_weight, up_weight, down_weight, norm_gain, query_weight):
    n_tok, width = tokens.shape
    hidden = gate_weight.shape[2]
    depth, cols, qcols = gate_weight.shape[1], down_weight.shape[2], query_weight.shape[1]
    experts = jnp.arange(2 * NZ, dtype=jnp.int32)
    named = routes[None, :, :] == experts[:, None, None]
    gtab = jnp.sum(jnp.where(named, route_gain[None, :, :], 0.0), axis=2)
    n_rows = 2 * NZ * n_tok
    vmem = pl.BlockSpec(memory_space=pltpu.VMEM)
    b16, f32 = jnp.bfloat16, jnp.float32
    dma = pltpu.SemaphoreType.DMA
    return pl.pallas_call(
        kernel,
        out_shape=(
            jax.ShapeDtypeStruct((n_tok, width), b16),
            jax.ShapeDtypeStruct((n_tok, 4 * qcols), b16),
        ),
        in_specs=[vmem] * 7,
        out_specs=(vmem, vmem),
        scratch_shapes=[
            pltpu.VMEM((n_rows, width), b16),
            pltpu.VMEM((2 * NZ, 2 * NZ, n_tok), f32),
            pltpu.VMEM((n_rows, n_tok), f32),
            pltpu.VMEM((3, depth, hidden), b16),
            pltpu.VMEM((3, depth, hidden), b16),
            pltpu.VMEM((3, hidden, cols), b16),
            pltpu.VMEM((3, width, qcols), b16),
            pltpu.VMEM((n_rows, hidden), f32),
            pltpu.VMEM((n_rows, hidden), f32),
            pltpu.VMEM((n_rows, hidden), b16),
            pltpu.VMEM((4, NZ, n_tok, cols), b16),
            pltpu.VMEM((4, NZ, n_tok, cols), b16),
            pltpu.VMEM((4, NZ, n_tok, cols), f32),
            pltpu.VMEM((4, NZ, n_tok, cols), b16),
            pltpu.VMEM((4, NZ, n_tok, cols), b16),
            pltpu.VMEM((4, NZ, n_tok, cols), b16),
            pltpu.VMEM((n_tok, width), f32),
            pltpu.VMEM((n_tok, width), b16),
            dma((2 * NZ,)),
            dma((2 * NZ,)),
            dma((2 * NZ,)),
            dma((NZ,)),
            dma((NZ,)),
            dma((NZ,)),
            dma((3, 4)),
            dma((3, 4)),
            dma((8,)),
            dma((8,)),
            dma((4,)),
            dma((4,)),
            dma((4, NZ)),
            dma((4, NZ)),
            dma((4, NZ)),
            dma((4, NZ)),
        ],
        compiler_params=pltpu.CompilerParams(
            collective_id=0, has_side_effects=True, vmem_limit_bytes=60 * 1024 * 1024
        ),
    )(
        tokens, gtab, gate_weight[0], up_weight[0], down_weight[0],
        norm_gain.reshape(1, width), query_weight,
    )


def general(
    tokens, routes, route_gain, gate_weight, up_weight, down_weight, norm_gain, query_weight
):
    ep_count = lax.axis_size("ep")
    tok_rows = tokens.shape[0]
    width = tokens.shape[1]
    choose = routes.shape[1]
    capacity = 8 * tok_rows // ep_count
    flat = routes.reshape(-1)
    onehot = (flat[:, None] == jnp.arange(ep_count, dtype=jnp.int32)[None, :]).astype(jnp.int32)
    counted = jnp.cumsum(onehot, axis=0)
    rank = jnp.sum(onehot * (counted - 1), axis=1)
    slot = flat * capacity + rank
    repeated = jnp.repeat(tokens, choose, axis=0)
    outbound = jnp.zeros((ep_count * capacity, width), jnp.bfloat16).at[slot].set(repeated)
    arrived = lax.all_to_all(outbound, "ep", split_axis=0, concat_axis=0, tiled=True)
    gate = jnp.dot(
        arrived,
        lax.all_gather(gate_weight[0], "grp", axis=0, tiled=True),
        preferred_element_type=jnp.float32,
    )
    up = jnp.dot(
        arrived,
        lax.all_gather(up_weight[0], "grp", axis=0, tiled=True),
        preferred_element_type=jnp.float32,
    )
    hidden = (jax.nn.silu(gate) * up).astype(jnp.bfloat16)
    answers = jnp.dot(
        hidden,
        lax.all_gather(down_weight[0], "grp", axis=1, tiled=True),
        preferred_element_type=jnp.float32,
    ).astype(jnp.bfloat16)
    returned = lax.all_to_all(answers, "ep", split_axis=0, concat_axis=0, tiled=True)
    picked = returned[slot].reshape(tok_rows, choose, width).astype(jnp.float32)
    total = tokens.astype(jnp.float32) + jnp.sum(picked * route_gain[:, :, None], axis=1)
    square = jnp.mean(total * total, axis=-1, keepdims=True)
    normed = (total * lax.rsqrt(square + 1e-06) * norm_gain).astype(jnp.bfloat16)
    query = jnp.dot(
        normed,
        lax.all_gather(query_weight, "grp", axis=1, tiled=True),
        preferred_element_type=jnp.float32,
    ).astype(jnp.bfloat16)
    return (total.astype(jnp.bfloat16), query)


def solution(mesh):
    placed = (
        P(("grp", "ep"), None),
        P(("grp", "ep"), None),
        P(("grp", "ep"), None),
        P("ep", "grp", None),
        P("ep", "grp", None),
        P("ep", None, "grp"),
        P(),
        P(None, "grp"),
    )
    small = mesh.shape["grp"] == 4 and mesh.shape["ep"] == 2 * NZ
    return jax.shard_map(
        fused if small else general,
        mesh=mesh,
        in_specs=placed,
        out_specs=(P(("grp", "ep"), None), P(("grp", "ep"), None)),
        check_vma=False,
    )
```

```python
import jax
import jax.numpy as jnp
from jax import lax
from jax.experimental import pallas as pl
from jax.experimental.pallas import tpu as pltpu
from jax.sharding import PartitionSpec as P

MESH = pl.DeviceIdType.MESH
NZ = 4


def kernel(
    tok, routes, gain, gw, uw, dw, ng, qw, mixed, query,
    rows, gtab, gains, scale, gin, uin, din, qin, acc_g, acc_u, hid,
    sout, sin, part, rin, lin, rout, total, normed,
    gain_s, gain_r, tok_r, tok_sr, tok_sl, tok_ss, w_s, w_r, q_s, q_r,
    sib_s, sib_r, right_s, right_r, left_s, left_r,
):
    g = lax.axis_index("grp")
    ep = lax.axis_index("ep")
    z = ep // 2
    c = ep % 2
    gx = g + 1 - 2 * (g % 2)
    gy = (g + 2) % 4
    gd = 3 - g
    x_dev, y_dev = (gx, ep), (gy, ep)
    sib = (g, ep + 1 - 2 * c)
    nxt, prv = (g, ep + 2), (g, ep - 2)
    n_tok, width = tok.shape
    depth = gw.shape[0]
    cols = dw.shape[1]
    qcols = qw.shape[1]
    has_next, has_prev = z < NZ - 1, z > 0

    def remote(src, dst, s, r, dev):
        return pltpu.make_async_remote_copy(
            src_ref=src, dst_ref=dst, send_sem=s, recv_sem=r, device_id=dev, device_id_type=MESH
        )

    barrier = pltpu.get_barrier_semaphore()
    for k in range(1, 2 * NZ):
        pl.semaphore_signal(barrier, inc=1, device_id=(g, (ep + k) % (2 * NZ)), device_id_type=MESH)
    for dev in (x_dev, y_dev):
        pl.semaphore_signal(barrier, inc=1, device_id=dev, device_id_type=MESH)
    pl.semaphore_wait(barrier, 2 * NZ + 1)

    def block(zz, cc):
        return rows.at[pl.ds(pl.multiple_of((cc * NZ + zz) * n_tok, n_tok), n_tok)]

    def tok_copy(src, zz, send, dev):
        return remote(src, block(zz, c), send.at[zz], tok_r.at[c * NZ + zz], dev)

    def tok_wait(zz, cc):
        ref = block(zz, cc)
        remote(ref, ref, tok_ss.at[0], tok_r.at[cc * NZ + zz], sib).wait_recv()

    @pl.when(has_next)
    def _():
        tok_copy(tok, z, tok_sr, nxt).start()

    @pl.when(has_prev)
    def _():
        tok_copy(tok, z, tok_sl, prv).start()

    tok_copy(tok, z, tok_ss, sib).start()

    shards_of = ((gw, gin), (uw, uin), (dw, din))

    def own_x(i):
        src, dst = shards_of[i]
        return remote(src, dst.at[0], w_s.at[i, 0], w_r.at[i, 0], x_dev)

    def own_y(i):
        src, dst = shards_of[i]
        return remote(src, dst.at[1], w_s.at[i, 1], w_r.at[i, 1], y_dev)

    def relay_y(i):
        dst = shards_of[i][1]
        half = dst.shape[1] // 2
        return remote(
            dst.at[0, pl.ds(0, half)], dst.at[2, pl.ds(0, half)], w_s.at[i, 2], w_r.at[i, 2], y_dev
        )

    def relay_x(i):
        dst = shards_of[i][1]
        half = dst.shape[1] // 2
        return remote(
            dst.at[1, pl.ds(half, half)], dst.at[2, pl.ds(half, half)],
            w_s.at[i, 3], w_r.at[i, 3], x_dev,
        )

    own_x(0).start()
    own_y(0).start()
    own_x(1).start()
    own_y(1).start()

    def gain_copy(k):
        return remote(
            gtab, gains.at[c * NZ + z], gain_s.at[k], gain_r.at[c * NZ + z],
            (g, (ep + k) % (2 * NZ)),
        )

    expert = lax.broadcasted_iota(jnp.int32, (2 * NZ, n_tok), 0)
    table = jnp.zeros((2 * NZ, n_tok), jnp.float32)
    for k in range(routes.shape[0]):
        table = table + jnp.where(expert == routes[k : k + 1, :], gain[k : k + 1, :], 0.0)
    gtab[...] = table
    for k in range(1, 2 * NZ):
        gain_copy(k).start()

    rows[pl.ds(pl.multiple_of((c * NZ + z) * n_tok, n_tok), n_tok), :] = tok[...]
    gains[c * NZ + z] = gtab[...]

    def hop(h):
        left, right = z - 1 - h, z + 1 + h

        @pl.when(left >= 0)
        def _():
            tok_wait(left, c)

            @pl.when(has_next)
            def _():
                tok_copy(block(left, c), left, tok_sr, nxt).start()

            tok_copy(block(left, c), left, tok_ss, sib).start()

        @pl.when(right <= NZ - 1)
        def _():
            tok_wait(right, c)

            @pl.when(has_prev)
            def _():
                tok_copy(block(right, c), right, tok_sl, prv).start()

            tok_copy(block(right, c), right, tok_ss, sib).start()

    def pass_on(i):
        own_x(i).wait_recv()
        relay_y(i).start()
        own_y(i).wait_recv()
        relay_x(i).start()

    hop(0)
    hop(1)
    pass_on(0)
    hop(2)
    pass_on(1)
    own_x(2).start()
    own_y(2).start()

    for k in range(1, 2 * NZ):
        peer = (ep + k) % (2 * NZ)
        at = (peer % 2) * NZ + peer // 2
        remote(gtab, gains.at[at], gain_s.at[0], gain_r.at[at], sib).wait_recv()
    for b in range(2 * NZ):
        table = gains[b]
        chosen = lax.broadcasted_iota(jnp.int32, table.shape, 0) == ep
        line = jnp.sum(jnp.where(chosen, table, 0.0), axis=0, keepdims=True)
        scale[b * n_tok : (b + 1) * n_tok, :] = jnp.broadcast_to(line, (n_tok, n_tok)).T
    for zz in range(NZ):
        tok_wait(zz, 1 - c)

    tile = 2 * n_tok
    tiles = rows.shape[0] // tile

    def partial(acc, w, owner, first):
        at = pl.ds(pl.multiple_of(owner * depth, depth), depth)

        def body(i, carry):
            r = pl.ds(pl.multiple_of(i * tile, tile), tile)
            p = jnp.dot(rows[r, at], w[...], preferred_element_type=jnp.float32)
            acc[r, :] = p if first else acc[r, :] + p
            return carry

        lax.fori_loop(0, tiles, body, 0)

    partial(acc_g, gw, g, True)
    partial(acc_u, uw, g, True)
    partial(acc_g, gin.at[0], gx, False)
    partial(acc_g, gin.at[1], gy, False)
    partial(acc_u, uin.at[0], gx, False)
    partial(acc_u, uin.at[1], gy, False)
    relay_y(0).wait_recv()
    relay_x(0).wait_recv()
    partial(acc_g, gin.at[2], gd, False)
    relay_y(1).wait_recv()
    relay_x(1).wait_recv()
    partial(acc_u, uin.at[2], gd, False)

    def act(i, carry):
        r = pl.ds(pl.multiple_of(i * n_tok, n_tok), n_tok)
        gate = acc_g[r, :]
        hid[r, :] = (gate / (1.0 + jnp.exp(-gate)) * acc_u[r, :]).astype(hid.dtype)
        return carry

    lax.fori_loop(0, rows.shape[0] // n_tok, act, 0)

    def sib_copy(q):
        return remote(sout.at[q], sin.at[q], sib_s.at[q], sib_r.at[q], sib)

    def answers(q, w):
        per = tile // n_tok

        def weighted(cc, i):
            at = pl.multiple_of(cc * NZ * n_tok + i * tile, tile)
            p = jnp.dot(hid[pl.ds(at, tile), :], w[...], preferred_element_type=jnp.float32)
            s = scale[pl.ds(at, tile), :]
            p = p * jnp.concatenate([s] * (cols // n_tok), axis=1)
            return p.reshape(per, n_tok, cols)

        def away(i, carry):
            sout[q, pl.ds(i * per, per)] = weighted(1 - c, i).astype(sout.dtype)
            return carry

        def here(i, carry):
            part[q, pl.ds(i * per, per)] = weighted(c, i)
            return carry

        lax.fori_loop(0, NZ // per, away, 0)
        sib_copy(q).start()
        lax.fori_loop(0, NZ // per, here, 0)
        sib_copy(q).wait_recv()

    def right_copy(q, d):
        return remote(rout.at[q, d], rin.at[q, d], right_s.at[q, d], right_r.at[q, d], nxt)

    def left_copy(q, d):
        return remote(rout.at[q, d], lin.at[q, d], left_s.at[q, d], left_r.at[q, d], prv)

    def ends(q):
        @pl.when(z == 0)
        def _():
            for d in range(NZ - 1, 0, -1):
                rout[q, d] = (part[q, d] + sin[q, d].astype(jnp.float32)).astype(rout.dtype)
                right_copy(q, d).start()

        @pl.when(z == NZ - 1)
        def _():
            for d in range(NZ - 1):
                rout[q, d] = (part[q, d] + sin[q, d].astype(jnp.float32)).astype(rout.dtype)
                left_copy(q, d).start()

    def chain(q, owner):
        for k in range(NZ - 1):
            d = NZ - 1 - k

            @pl.when((z > 0) & (z < d))
            def _():
                right_copy(q, d).wait_recv()
                rout[q, d] = (
                    part[q, d] + sin[q, d].astype(jnp.float32) + rin[q, d].astype(jnp.float32)
                ).astype(rout.dtype)
                right_copy(q, d).start()

            @pl.when((z < NZ - 1) & (z > k))
            def _():
                left_copy(q, k).wait_recv()
                rout[q, k] = (
                    part[q, k] + sin[q, k].astype(jnp.float32) + lin[q, k].astype(jnp.float32)
                ).astype(rout.dtype)
                left_copy(q, k).start()

        at = pl.ds(pl.multiple_of(owner * cols, cols), cols)
        total[:, at] = tok[:, at].astype(jnp.float32) + part[q, z] + sin[q, z].astype(jnp.float32)

        @pl.when(has_prev)
        def _():
            right_copy(q, z).wait_recv()
            total[:, at] = total[:, at] + rin[q, z].astype(jnp.float32)

        @pl.when(has_next)
        def _():
            left_copy(q, z).wait_recv()
            total[:, at] = total[:, at] + lin[q, z].astype(jnp.float32)

    q_half = qw.shape[0] // 2
    q_quarter = q_half // 2
    half_at = pl.ds(pl.multiple_of(c * q_half, q_half), q_half)
    first_at = pl.ds(pl.multiple_of(c * q_half, q_quarter), q_quarter)
    second_at = pl.ds(pl.multiple_of(c * q_half + q_quarter, q_quarter), q_quarter)

    def q_copy(k):
        if k == 0:
            return remote(qw.at[half_at], qin.at[0, half_at], q_s.at[0], q_r.at[0], x_dev)
        if k == 1:
            return remote(qw.at[half_at], qin.at[1, half_at], q_s.at[1], q_r.at[1], y_dev)
        if k == 2:
            return remote(qin.at[0, first_at], qin.at[2, first_at], q_s.at[2], q_r.at[2], y_dev)
        if k == 3:
            return remote(qin.at[1, second_at], qin.at[2, second_at], q_s.at[3], q_r.at[3], x_dev)
        slot, at = ((0, half_at), (1, half_at), (2, first_at), (2, second_at))[k - 4]
        return remote(qin.at[slot, at], qin.at[slot, at], q_s.at[k], q_r.at[k], sib)

    other_half = pl.ds(pl.multiple_of((1 - c) * q_half, q_half), q_half)
    other_first = pl.ds(pl.multiple_of((1 - c) * q_half, q_quarter), q_quarter)
    other_second = pl.ds(pl.multiple_of((1 - c) * q_half + q_quarter, q_quarter), q_quarter)

    def q_wait_sib(k):
        slot, at = ((0, other_half), (1, other_half), (2, other_first), (2, other_second))[k - 4]
        remote(qin.at[slot, at], qin.at[slot, at], q_s.at[k], q_r.at[k], sib).wait_recv()

    answers(0, dw)
    ends(0)
    pass_on(2)
    q_copy(0).start()
    q_copy(1).start()
    chain(0, g)
    answers(1, din.at[0])
    ends(1)
    answers(2, din.at[1])
    ends(2)
    chain(1, gx)
    relay_y(2).wait_recv()
    relay_x(2).wait_recv()
    answers(3, din.at[2])
    ends(3)
    chain(2, gy)
    q_copy(0).wait_recv()
    q_copy(2).start()
    q_copy(4).start()
    q_copy(1).wait_recv()
    q_copy(3).start()
    q_copy(5).start()
    chain(3, gd)

    value = total[...]
    mixed[...] = value.astype(mixed.dtype)
    square = jnp.sum(value * value, axis=-1, keepdims=True) * (1.0 / width)
    normed[...] = (value * lax.rsqrt(square + 1e-06) * ng[...]).astype(normed.dtype)

    def project(w, owner):
        at = pl.ds(pl.multiple_of(owner * qcols, qcols), qcols)
        query[:, at] = jnp.dot(
            normed[...], w[...], preferred_element_type=jnp.float32
        ).astype(query.dtype)

    project(qw, g)
    q_wait_sib(4)
    project(qin.at[0], gx)
    q_wait_sib(5)
    project(qin.at[1], gy)
    q_copy(2).wait_recv()
    q_copy(6).start()
    q_copy(3).wait_recv()
    q_copy(7).start()
    q_wait_sib(6)
    q_wait_sib(7)
    project(qin.at[2], gd)

    for k in range(1, 2 * NZ):
        gain_copy(k).wait_send()
    for zz in range(NZ):
        @pl.when(has_next & (zz <= z))
        def _():
            tok_copy(tok, zz, tok_sr, nxt).wait_send()

        @pl.when(has_prev & (zz >= z))
        def _():
            tok_copy(tok, zz, tok_sl, prv).wait_send()

        tok_copy(tok, zz, tok_ss, sib).wait_send()
    for i in range(3):
        for copy in (own_x, own_y, relay_x, relay_y):
            copy(i).wait_send()
    for k in range(8):
        q_copy(k).wait_send()
    for q in range(4):
        sib_copy(q).wait_send()
        for d in range(NZ):
            if d > 0:
                @pl.when(z < d)
                def _():
                    right_copy(q, d).wait_send()
            if d < NZ - 1:
                @pl.when(z > d)
                def _():
                    left_copy(q, d).wait_send()


def fused(tokens, routes, route_gain, gate_weight, up_weight, down_weight, norm_gain, query_weight):
    n_tok, width = tokens.shape
    hidden = gate_weight.shape[2]
    depth, cols, qcols = gate_weight.shape[1], down_weight.shape[2], query_weight.shape[1]
    n_rows = 2 * NZ * n_tok
    vmem = pl.BlockSpec(memory_space=pltpu.VMEM)
    b16, f32 = jnp.bfloat16, jnp.float32
    dma = pltpu.SemaphoreType.DMA
    return pl.pallas_call(
        kernel,
        out_shape=(
            jax.ShapeDtypeStruct((n_tok, width), b16),
            jax.ShapeDtypeStruct((n_tok, 4 * qcols), b16),
        ),
        in_specs=[vmem] * 8,
        out_specs=(vmem, vmem),
        scratch_shapes=[
            pltpu.VMEM((n_rows, width), b16),
            pltpu.VMEM((2 * NZ, n_tok), f32),
            pltpu.VMEM((2 * NZ, 2 * NZ, n_tok), f32),
            pltpu.VMEM((n_rows, n_tok), f32),
            pltpu.VMEM((3, depth, hidden), b16),
            pltpu.VMEM((3, depth, hidden), b16),
            pltpu.VMEM((3, hidden, cols), b16),
            pltpu.VMEM((3, width, qcols), b16),
            pltpu.VMEM((n_rows, hidden), f32),
            pltpu.VMEM((n_rows, hidden), f32),
            pltpu.VMEM((n_rows, hidden), b16),
            pltpu.VMEM((4, NZ, n_tok, cols), b16),
            pltpu.VMEM((4, NZ, n_tok, cols), b16),
            pltpu.VMEM((4, NZ, n_tok, cols), f32),
            pltpu.VMEM((4, NZ, n_tok, cols), b16),
            pltpu.VMEM((4, NZ, n_tok, cols), b16),
            pltpu.VMEM((4, NZ, n_tok, cols), b16),
            pltpu.VMEM((n_tok, width), f32),
            pltpu.VMEM((n_tok, width), b16),
            dma((2 * NZ,)),
            dma((2 * NZ,)),
            dma((2 * NZ,)),
            dma((NZ,)),
            dma((NZ,)),
            dma((NZ,)),
            dma((3, 4)),
            dma((3, 4)),
            dma((8,)),
            dma((8,)),
            dma((4,)),
            dma((4,)),
            dma((4, NZ)),
            dma((4, NZ)),
            dma((4, NZ)),
            dma((4, NZ)),
        ],
        compiler_params=pltpu.CompilerParams(
            collective_id=0, has_side_effects=True, vmem_limit_bytes=60 * 1024 * 1024
        ),
    )(
        tokens, routes.T, route_gain.T, gate_weight[0], up_weight[0], down_weight[0],
        norm_gain.reshape(1, width), query_weight,
    )


def general(
    tokens, routes, route_gain, gate_weight, up_weight, down_weight, norm_gain, query_weight
):
    ep_count = lax.axis_size("ep")
    tok_rows = tokens.shape[0]
    width = tokens.shape[1]
    choose = routes.shape[1]
    capacity = 8 * tok_rows // ep_count
    flat = routes.reshape(-1)
    onehot = (flat[:, None] == jnp.arange(ep_count, dtype=jnp.int32)[None, :]).astype(jnp.int32)
    counted = jnp.cumsum(onehot, axis=0)
    rank = jnp.sum(onehot * (counted - 1), axis=1)
    slot = flat * capacity + rank
    repeated = jnp.repeat(tokens, choose, axis=0)
    outbound = jnp.zeros((ep_count * capacity, width), jnp.bfloat16).at[slot].set(repeated)
    arrived = lax.all_to_all(outbound, "ep", split_axis=0, concat_axis=0, tiled=True)
    gate = jnp.dot(
        arrived,
        lax.all_gather(gate_weight[0], "grp", axis=0, tiled=True),
        preferred_element_type=jnp.float32,
    )
    up = jnp.dot(
        arrived,
        lax.all_gather(up_weight[0], "grp", axis=0, tiled=True),
        preferred_element_type=jnp.float32,
    )
    hidden = (jax.nn.silu(gate) * up).astype(jnp.bfloat16)
    answers = jnp.dot(
        hidden,
        lax.all_gather(down_weight[0], "grp", axis=1, tiled=True),
        preferred_element_type=jnp.float32,
    ).astype(jnp.bfloat16)
    returned = lax.all_to_all(answers, "ep", split_axis=0, concat_axis=0, tiled=True)
    picked = returned[slot].reshape(tok_rows, choose, width).astype(jnp.float32)
    total = tokens.astype(jnp.float32) + jnp.sum(picked * route_gain[:, :, None], axis=1)
    square = jnp.mean(total * total, axis=-1, keepdims=True)
    normed = (total * lax.rsqrt(square + 1e-06) * norm_gain).astype(jnp.bfloat16)
    query = jnp.dot(
        normed,
        lax.all_gather(query_weight, "grp", axis=1, tiled=True),
        preferred_element_type=jnp.float32,
    ).astype(jnp.bfloat16)
    return (total.astype(jnp.bfloat16), query)


def solution(mesh):
    placed = (
        P(("grp", "ep"), None),
        P(("grp", "ep"), None),
        P(("grp", "ep"), None),
        P("ep", "grp", None),
        P("ep", "grp", None),
        P("ep", None, "grp"),
        P(),
        P(None, "grp"),
    )
    small = mesh.shape["grp"] == 4 and mesh.shape["ep"] == 2 * NZ
    return jax.shard_map(
        fused if small else general,
        mesh=mesh,
        in_specs=placed,
        out_specs=(P(("grp", "ep"), None), P(("grp", "ep"), None)),
        check_vma=False,
    )
```

```python
import jax
import jax.numpy as jnp
from jax import lax
from jax.experimental import pallas as pl
from jax.experimental.pallas import tpu as pltpu
from jax.sharding import PartitionSpec as P

MESH = pl.DeviceIdType.MESH
NZ = 4


def kernel(
    tok, routes, gain, gw, uw, dw, ng, qw, mixed, query,
    rows, gtab, gains, scale, gin, uin, din, qin, acc_g, acc_u, hid,
    sout, sin, part, rin, lin, rout, total, normed,
    gain_s, gain_r, tok_r, tok_sr, tok_sl, tok_ss, w_s, w_r, q_s, q_r,
    sib_s, sib_r, right_s, right_r, left_s, left_r,
):
    g = lax.axis_index("grp")
    ep = lax.axis_index("ep")
    z = ep // 2
    c = ep % 2
    gx = g + 1 - 2 * (g % 2)
    gy = (g + 2) % 4
    gd = 3 - g
    x_dev, y_dev = (gx, ep), (gy, ep)
    sib = (g, ep + 1 - 2 * c)
    nxt, prv = (g, ep + 2), (g, ep - 2)
    n_tok, width = tok.shape
    depth = gw.shape[0]
    cols = dw.shape[1]
    qcols = qw.shape[1]
    has_next, has_prev = z < NZ - 1, z > 0

    def remote(src, dst, s, r, dev):
        return pltpu.make_async_remote_copy(
            src_ref=src, dst_ref=dst, send_sem=s, recv_sem=r, device_id=dev, device_id_type=MESH
        )

    barrier = pltpu.get_barrier_semaphore()
    for k in range(1, 2 * NZ):
        pl.semaphore_signal(barrier, inc=1, device_id=(g, (ep + k) % (2 * NZ)), device_id_type=MESH)
    for dev in (x_dev, y_dev):
        pl.semaphore_signal(barrier, inc=1, device_id=dev, device_id_type=MESH)
    pl.semaphore_wait(barrier, 2 * NZ + 1)

    def block(zz, cc):
        return rows.at[pl.ds(pl.multiple_of((cc * NZ + zz) * n_tok, n_tok), n_tok)]

    def tok_copy(src, zz, send, dev):
        return remote(src, block(zz, c), send.at[zz], tok_r.at[c * NZ + zz], dev)

    def tok_wait(zz, cc):
        ref = block(zz, cc)
        remote(ref, ref, tok_ss.at[0], tok_r.at[cc * NZ + zz], sib).wait_recv()

    @pl.when(has_next)
    def _():
        tok_copy(tok, z, tok_sr, nxt).start()

    @pl.when(has_prev)
    def _():
        tok_copy(tok, z, tok_sl, prv).start()

    tok_copy(tok, z, tok_ss, sib).start()

    shards_of = ((gw, gin), (uw, uin), (dw, din))

    def own_x(i):
        src, dst = shards_of[i]
        return remote(src, dst.at[0], w_s.at[i, 0], w_r.at[i, 0], x_dev)

    def own_y(i):
        src, dst = shards_of[i]
        return remote(src, dst.at[1], w_s.at[i, 1], w_r.at[i, 1], y_dev)

    def relay_y(i):
        dst = shards_of[i][1]
        half = dst.shape[1] // 2
        return remote(
            dst.at[0, pl.ds(0, half)], dst.at[2, pl.ds(0, half)], w_s.at[i, 2], w_r.at[i, 2], y_dev
        )

    def relay_x(i):
        dst = shards_of[i][1]
        half = dst.shape[1] // 2
        return remote(
            dst.at[1, pl.ds(half, half)], dst.at[2, pl.ds(half, half)],
            w_s.at[i, 3], w_r.at[i, 3], x_dev,
        )

    own_x(0).start()
    own_y(0).start()
    own_x(1).start()
    own_y(1).start()

    def gain_copy(k):
        return remote(
            gtab, gains.at[c * NZ + z], gain_s.at[k], gain_r.at[c * NZ + z],
            (g, (ep + k) % (2 * NZ)),
        )

    expert = lax.broadcasted_iota(jnp.int32, (2 * NZ, n_tok), 0)
    table = jnp.zeros((2 * NZ, n_tok), jnp.float32)
    for k in range(routes.shape[0]):
        table = table + jnp.where(expert == routes[k : k + 1, :], gain[k : k + 1, :], 0.0)
    gtab[...] = table
    for k in range(1, 2 * NZ):
        gain_copy(k).start()

    rows[pl.ds(pl.multiple_of((c * NZ + z) * n_tok, n_tok), n_tok), :] = tok[...]
    gains[c * NZ + z] = gtab[...]

    def hop(h):
        left, right = z - 1 - h, z + 1 + h

        @pl.when(left >= 0)
        def _():
            tok_wait(left, c)

            @pl.when(has_next)
            def _():
                tok_copy(block(left, c), left, tok_sr, nxt).start()

            tok_copy(block(left, c), left, tok_ss, sib).start()

        @pl.when(right <= NZ - 1)
        def _():
            tok_wait(right, c)

            @pl.when(has_prev)
            def _():
                tok_copy(block(right, c), right, tok_sl, prv).start()

            tok_copy(block(right, c), right, tok_ss, sib).start()

    def pass_on(i):
        own_x(i).wait_recv()
        relay_y(i).start()
        own_y(i).wait_recv()
        relay_x(i).start()

    hop(0)
    hop(1)
    pass_on(0)
    hop(2)
    pass_on(1)

    for k in range(1, 2 * NZ):
        peer = (ep + k) % (2 * NZ)
        at = (peer % 2) * NZ + peer // 2
        remote(gtab, gains.at[at], gain_s.at[0], gain_r.at[at], sib).wait_recv()
    for b in range(2 * NZ):
        table = gains[b]
        chosen = lax.broadcasted_iota(jnp.int32, table.shape, 0) == ep
        line = jnp.sum(jnp.where(chosen, table, 0.0), axis=0, keepdims=True)
        scale[b * n_tok : (b + 1) * n_tok, :] = jnp.broadcast_to(line, (n_tok, n_tok)).T
    for zz in range(NZ):
        tok_wait(zz, 1 - c)

    tile = 2 * n_tok
    tiles = rows.shape[0] // tile

    def partial(acc, w, owner, first):
        at = pl.ds(pl.multiple_of(owner * depth, depth), depth)

        def body(i, carry):
            r = pl.ds(pl.multiple_of(i * tile, tile), tile)
            p = jnp.dot(rows[r, at], w[...], preferred_element_type=jnp.float32)
            acc[r, :] = p if first else acc[r, :] + p
            return carry

        lax.fori_loop(0, tiles, body, 0)

    partial(acc_g, gw, g, True)
    partial(acc_u, uw, g, True)
    partial(acc_g, gin.at[0], gx, False)
    partial(acc_g, gin.at[1], gy, False)
    partial(acc_u, uin.at[0], gx, False)
    partial(acc_u, uin.at[1], gy, False)
    relay_y(0).wait_recv()
    relay_x(0).wait_recv()
    own_x(2).start()
    own_y(2).start()
    partial(acc_g, gin.at[2], gd, False)
    relay_y(1).wait_recv()
    relay_x(1).wait_recv()
    partial(acc_u, uin.at[2], gd, False)

    def act(i, carry):
        r = pl.ds(pl.multiple_of(i * n_tok, n_tok), n_tok)
        gate = acc_g[r, :]
        hid[r, :] = (gate / (1.0 + jnp.exp(-gate)) * acc_u[r, :]).astype(hid.dtype)
        return carry

    lax.fori_loop(0, rows.shape[0] // n_tok, act, 0)

    def sib_copy(q):
        return remote(sout.at[q], sin.at[q], sib_s.at[q], sib_r.at[q], sib)

    def answers(q, w):
        per = tile // n_tok

        def weighted(cc, i):
            at = pl.multiple_of(cc * NZ * n_tok + i * tile, tile)
            p = jnp.dot(hid[pl.ds(at, tile), :], w[...], preferred_element_type=jnp.float32)
            s = scale[pl.ds(at, tile), :]
            p = p * jnp.concatenate([s] * (cols // n_tok), axis=1)
            return p.reshape(per, n_tok, cols)

        def away(i, carry):
            sout[q, pl.ds(i * per, per)] = weighted(1 - c, i).astype(sout.dtype)
            return carry

        def here(i, carry):
            part[q, pl.ds(i * per, per)] = weighted(c, i)
            return carry

        lax.fori_loop(0, NZ // per, away, 0)
        sib_copy(q).start()
        lax.fori_loop(0, NZ // per, here, 0)
        sib_copy(q).wait_recv()

    def right_copy(q, d):
        return remote(rout.at[q, d], rin.at[q, d], right_s.at[q, d], right_r.at[q, d], nxt)

    def left_copy(q, d):
        return remote(rout.at[q, d], lin.at[q, d], left_s.at[q, d], left_r.at[q, d], prv)

    def ends(q):
        @pl.when(z == 0)
        def _():
            for d in range(NZ - 1, 0, -1):
                rout[q, d] = (part[q, d] + sin[q, d].astype(jnp.float32)).astype(rout.dtype)
                right_copy(q, d).start()

        @pl.when(z == NZ - 1)
        def _():
            for d in range(NZ - 1):
                rout[q, d] = (part[q, d] + sin[q, d].astype(jnp.float32)).astype(rout.dtype)
                left_copy(q, d).start()

    def go_right(q, d):
        right_copy(q, d).wait_recv()
        rout[q, d] = (
            part[q, d] + sin[q, d].astype(jnp.float32) + rin[q, d].astype(jnp.float32)
        ).astype(rout.dtype)
        right_copy(q, d).start()

    def go_left(q, d):
        left_copy(q, d).wait_recv()
        rout[q, d] = (
            part[q, d] + sin[q, d].astype(jnp.float32) + lin[q, d].astype(jnp.float32)
        ).astype(rout.dtype)
        left_copy(q, d).start()

    def near(q):
        @pl.when(z == 1)
        def _():
            for d in range(NZ - 1, 1, -1):
                go_right(q, d)

        @pl.when(z == NZ - 2)
        def _():
            for d in range(NZ - 2):
                go_left(q, d)

    def far(q):
        @pl.when(z == NZ - 2)
        def _():
            go_right(q, NZ - 1)

        @pl.when(z == 1)
        def _():
            go_left(q, 0)

    def finish(q, owner):
        at = pl.ds(pl.multiple_of(owner * cols, cols), cols)
        total[:, at] = tok[:, at].astype(jnp.float32) + part[q, z] + sin[q, z].astype(jnp.float32)

        @pl.when(has_prev)
        def _():
            right_copy(q, z).wait_recv()
            total[:, at] = total[:, at] + rin[q, z].astype(jnp.float32)

        @pl.when(has_next)
        def _():
            left_copy(q, z).wait_recv()
            total[:, at] = total[:, at] + lin[q, z].astype(jnp.float32)

    q_half = qw.shape[0] // 2
    q_quarter = q_half // 2
    half_at = pl.ds(pl.multiple_of(c * q_half, q_half), q_half)
    first_at = pl.ds(pl.multiple_of(c * q_half, q_quarter), q_quarter)
    second_at = pl.ds(pl.multiple_of(c * q_half + q_quarter, q_quarter), q_quarter)

    def q_copy(k):
        if k == 0:
            return remote(qw.at[half_at], qin.at[0, half_at], q_s.at[0], q_r.at[0], x_dev)
        if k == 1:
            return remote(qw.at[half_at], qin.at[1, half_at], q_s.at[1], q_r.at[1], y_dev)
        if k == 2:
            return remote(qin.at[0, first_at], qin.at[2, first_at], q_s.at[2], q_r.at[2], y_dev)
        if k == 3:
            return remote(qin.at[1, second_at], qin.at[2, second_at], q_s.at[3], q_r.at[3], x_dev)
        slot, at = ((0, half_at), (1, half_at), (2, first_at), (2, second_at))[k - 4]
        return remote(qin.at[slot, at], qin.at[slot, at], q_s.at[k], q_r.at[k], sib)

    other_half = pl.ds(pl.multiple_of((1 - c) * q_half, q_half), q_half)
    other_first = pl.ds(pl.multiple_of((1 - c) * q_half, q_quarter), q_quarter)
    other_second = pl.ds(pl.multiple_of((1 - c) * q_half + q_quarter, q_quarter), q_quarter)

    def q_wait_sib(k):
        slot, at = ((0, other_half), (1, other_half), (2, other_first), (2, other_second))[k - 4]
        remote(qin.at[slot, at], qin.at[slot, at], q_s.at[k], q_r.at[k], sib).wait_recv()

    answers(0, dw)
    ends(0)
    pass_on(2)
    near(0)
    answers(1, din.at[0])
    ends(1)
    far(0)
    answers(2, din.at[1])
    ends(2)
    near(1)
    relay_y(2).wait_recv()
    relay_x(2).wait_recv()
    q_copy(0).start()
    q_copy(1).start()
    answers(3, din.at[2])
    ends(3)
    far(1)
    near(2)
    far(2)
    near(3)
    q_copy(0).wait_recv()
    q_copy(2).start()
    q_copy(4).start()
    q_copy(1).wait_recv()
    q_copy(3).start()
    q_copy(5).start()
    far(3)
    finish(0, g)
    finish(1, gx)
    finish(2, gy)
    finish(3, gd)

    value = total[...]
    mixed[...] = value.astype(mixed.dtype)
    square = jnp.sum(value * value, axis=-1, keepdims=True) * (1.0 / width)
    normed[...] = (value * lax.rsqrt(square + 1e-06) * ng[...]).astype(normed.dtype)

    def project(w, owner):
        at = pl.ds(pl.multiple_of(owner * qcols, qcols), qcols)
        query[:, at] = jnp.dot(
            normed[...], w[...], preferred_element_type=jnp.float32
        ).astype(query.dtype)

    project(qw, g)
    q_wait_sib(4)
    project(qin.at[0], gx)
    q_wait_sib(5)
    project(qin.at[1], gy)
    q_copy(2).wait_recv()
    q_copy(6).start()
    q_copy(3).wait_recv()
    q_copy(7).start()
    q_wait_sib(6)
    q_wait_sib(7)
    project(qin.at[2], gd)

    for k in range(1, 2 * NZ):
        gain_copy(k).wait_send()
    for zz in range(NZ):
        @pl.when(has_next & (zz <= z))
        def _():
            tok_copy(tok, zz, tok_sr, nxt).wait_send()

        @pl.when(has_prev & (zz >= z))
        def _():
            tok_copy(tok, zz, tok_sl, prv).wait_send()

        tok_copy(tok, zz, tok_ss, sib).wait_send()
    for i in range(3):
        for copy in (own_x, own_y, relay_x, relay_y):
            copy(i).wait_send()
    for k in range(8):
        q_copy(k).wait_send()
    for q in range(4):
        sib_copy(q).wait_send()
        for d in range(NZ):
            if d > 0:
                @pl.when(z < d)
                def _():
                    right_copy(q, d).wait_send()
            if d < NZ - 1:
                @pl.when(z > d)
                def _():
                    left_copy(q, d).wait_send()


def fused(tokens, routes, route_gain, gate_weight, up_weight, down_weight, norm_gain, query_weight):
    n_tok, width = tokens.shape
    hidden = gate_weight.shape[2]
    depth, cols, qcols = gate_weight.shape[1], down_weight.shape[2], query_weight.shape[1]
    n_rows = 2 * NZ * n_tok
    vmem = pl.BlockSpec(memory_space=pltpu.VMEM)
    b16, f32 = jnp.bfloat16, jnp.float32
    dma = pltpu.SemaphoreType.DMA
    return pl.pallas_call(
        kernel,
        out_shape=(
            jax.ShapeDtypeStruct((n_tok, width), b16),
            jax.ShapeDtypeStruct((n_tok, 4 * qcols), b16),
        ),
        in_specs=[vmem] * 8,
        out_specs=(vmem, vmem),
        scratch_shapes=[
            pltpu.VMEM((n_rows, width), b16),
            pltpu.VMEM((2 * NZ, n_tok), f32),
            pltpu.VMEM((2 * NZ, 2 * NZ, n_tok), f32),
            pltpu.VMEM((n_rows, n_tok), f32),
            pltpu.VMEM((3, depth, hidden), b16),
            pltpu.VMEM((3, depth, hidden), b16),
            pltpu.VMEM((3, hidden, cols), b16),
            pltpu.VMEM((3, width, qcols), b16),
            pltpu.VMEM((n_rows, hidden), f32),
            pltpu.VMEM((n_rows, hidden), f32),
            pltpu.VMEM((n_rows, hidden), b16),
            pltpu.VMEM((4, NZ, n_tok, cols), b16),
            pltpu.VMEM((4, NZ, n_tok, cols), b16),
            pltpu.VMEM((4, NZ, n_tok, cols), f32),
            pltpu.VMEM((4, NZ, n_tok, cols), b16),
            pltpu.VMEM((4, NZ, n_tok, cols), b16),
            pltpu.VMEM((4, NZ, n_tok, cols), b16),
            pltpu.VMEM((n_tok, width), f32),
            pltpu.VMEM((n_tok, width), b16),
            dma((2 * NZ,)),
            dma((2 * NZ,)),
            dma((2 * NZ,)),
            dma((NZ,)),
            dma((NZ,)),
            dma((NZ,)),
            dma((3, 4)),
            dma((3, 4)),
            dma((8,)),
            dma((8,)),
            dma((4,)),
            dma((4,)),
            dma((4, NZ)),
            dma((4, NZ)),
            dma((4, NZ)),
            dma((4, NZ)),
        ],
        compiler_params=pltpu.CompilerParams(
            collective_id=0, has_side_effects=True, vmem_limit_bytes=60 * 1024 * 1024
        ),
    )(
        tokens, routes.T, route_gain.T, gate_weight[0], up_weight[0], down_weight[0],
        norm_gain.reshape(1, width), query_weight,
    )


def general(
    tokens, routes, route_gain, gate_weight, up_weight, down_weight, norm_gain, query_weight
):
    ep_count = lax.axis_size("ep")
    tok_rows = tokens.shape[0]
    width = tokens.shape[1]
    choose = routes.shape[1]
    capacity = 8 * tok_rows // ep_count
    flat = routes.reshape(-1)
    onehot = (flat[:, None] == jnp.arange(ep_count, dtype=jnp.int32)[None, :]).astype(jnp.int32)
    counted = jnp.cumsum(onehot, axis=0)
    rank = jnp.sum(onehot * (counted - 1), axis=1)
    slot = flat * capacity + rank
    repeated = jnp.repeat(tokens, choose, axis=0)
    outbound = jnp.zeros((ep_count * capacity, width), jnp.bfloat16).at[slot].set(repeated)
    arrived = lax.all_to_all(outbound, "ep", split_axis=0, concat_axis=0, tiled=True)
    gate = jnp.dot(
        arrived,
        lax.all_gather(gate_weight[0], "grp", axis=0, tiled=True),
        preferred_element_type=jnp.float32,
    )
    up = jnp.dot(
        arrived,
        lax.all_gather(up_weight[0], "grp", axis=0, tiled=True),
        preferred_element_type=jnp.float32,
    )
    hidden = (jax.nn.silu(gate) * up).astype(jnp.bfloat16)
    answers = jnp.dot(
        hidden,
        lax.all_gather(down_weight[0], "grp", axis=1, tiled=True),
        preferred_element_type=jnp.float32,
    ).astype(jnp.bfloat16)
    returned = lax.all_to_all(answers, "ep", split_axis=0, concat_axis=0, tiled=True)
    picked = returned[slot].reshape(tok_rows, choose, width).astype(jnp.float32)
    total = tokens.astype(jnp.float32) + jnp.sum(picked * route_gain[:, :, None], axis=1)
    square = jnp.mean(total * total, axis=-1, keepdims=True)
    normed = (total * lax.rsqrt(square + 1e-06) * norm_gain).astype(jnp.bfloat16)
    query = jnp.dot(
        normed,
        lax.all_gather(query_weight, "grp", axis=1, tiled=True),
        preferred_element_type=jnp.float32,
    ).astype(jnp.bfloat16)
    return (total.astype(jnp.bfloat16), query)


def solution(mesh):
    placed = (
        P(("grp", "ep"), None),
        P(("grp", "ep"), None),
        P(("grp", "ep"), None),
        P("ep", "grp", None),
        P("ep", "grp", None),
        P("ep", None, "grp"),
        P(),
        P(None, "grp"),
    )
    small = mesh.shape["grp"] == 4 and mesh.shape["ep"] == 2 * NZ
    return jax.shard_map(
        fused if small else general,
        mesh=mesh,
        in_specs=placed,
        out_specs=(P(("grp", "ep"), None), P(("grp", "ep"), None)),
        check_vma=False,
    )
```

```python
import jax
import jax.numpy as jnp
from jax import lax
from jax.experimental import pallas as pl
from jax.experimental.pallas import tpu as pltpu
from jax.sharding import PartitionSpec as P

MESH = pl.DeviceIdType.MESH
NZ = 4


def kernel(
    tok, routes, gain, gw_far, uw_far, dw_far, ng, qw_far, mixed, query,
    gw, uw, dw, qw,
    rows, gtab, gains, scale, gin, uin, din, qin, acc_g, acc_u, hid,
    sout, sin, part, rin, lin, rout, total, normed,
    gain_s, gain_r, tok_r, tok_sr, tok_sl, tok_ss, w_s, w_r, q_s, q_r,
    sib_s, sib_r, right_s, right_r, left_s, left_r, own_r,
):
    g = lax.axis_index("grp")
    ep = lax.axis_index("ep")
    z = ep // 2
    c = ep % 2
    gx = g + 1 - 2 * (g % 2)
    gy = (g + 2) % 4
    gd = 3 - g
    x_dev, y_dev = (gx, ep), (gy, ep)
    sib = (g, ep + 1 - 2 * c)
    nxt, prv = (g, ep + 2), (g, ep - 2)
    n_tok, width = tok.shape
    depth = gw.shape[0]
    cols = dw.shape[1]
    qcols = qw.shape[1]
    has_next, has_prev = z < NZ - 1, z > 0

    def remote(src, dst, s, r, dev):
        return pltpu.make_async_remote_copy(
            src_ref=src, dst_ref=dst, send_sem=s, recv_sem=r, device_id=dev, device_id_type=MESH
        )

    barrier = pltpu.get_barrier_semaphore()
    for k in range(1, 2 * NZ):
        pl.semaphore_signal(barrier, inc=1, device_id=(g, (ep + k) % (2 * NZ)), device_id_type=MESH)
    for dev in (x_dev, y_dev):
        pl.semaphore_signal(barrier, inc=1, device_id=dev, device_id_type=MESH)
    pl.semaphore_wait(barrier, 2 * NZ + 1)

    def block(zz, cc):
        return rows.at[pl.ds(pl.multiple_of((cc * NZ + zz) * n_tok, n_tok), n_tok)]

    def tok_copy(src, zz, send, dev):
        return remote(src, block(zz, c), send.at[zz], tok_r.at[c * NZ + zz], dev)

    def tok_wait(zz, cc):
        ref = block(zz, cc)
        remote(ref, ref, tok_ss.at[0], tok_r.at[cc * NZ + zz], sib).wait_recv()

    @pl.when(has_next)
    def _():
        tok_copy(tok, z, tok_sr, nxt).start()

    @pl.when(has_prev)
    def _():
        tok_copy(tok, z, tok_sl, prv).start()

    tok_copy(tok, z, tok_ss, sib).start()

    shards_of = ((gw_far, gin), (uw_far, uin), (dw_far, din))

    def own_x(i):
        src, dst = shards_of[i]
        return remote(src, dst.at[0], w_s.at[i, 0], w_r.at[i, 0], x_dev)

    def own_y(i):
        src, dst = shards_of[i]
        return remote(src, dst.at[1], w_s.at[i, 1], w_r.at[i, 1], y_dev)

    def relay_y(i):
        dst = shards_of[i][1]
        half = dst.shape[1] // 2
        return remote(
            dst.at[0, pl.ds(0, half)], dst.at[2, pl.ds(0, half)], w_s.at[i, 2], w_r.at[i, 2], y_dev
        )

    def relay_x(i):
        dst = shards_of[i][1]
        half = dst.shape[1] // 2
        return remote(
            dst.at[1, pl.ds(half, half)], dst.at[2, pl.ds(half, half)],
            w_s.at[i, 3], w_r.at[i, 3], x_dev,
        )

    own_x(0).start()
    own_y(0).start()
    own_x(1).start()
    own_y(1).start()

    def fetch(i):
        src, dst = ((gw_far, gw), (uw_far, uw), (dw_far, dw), (qw_far, qw))[i]
        return pltpu.make_async_copy(src, dst, own_r.at[i])

    for i in range(4):
        fetch(i).start()

    def gain_copy(k):
        return remote(
            gtab, gains.at[c * NZ + z], gain_s.at[k], gain_r.at[c * NZ + z],
            (g, (ep + k) % (2 * NZ)),
        )

    expert = lax.broadcasted_iota(jnp.int32, (2 * NZ, n_tok), 0)
    table = jnp.zeros((2 * NZ, n_tok), jnp.float32)
    for k in range(routes.shape[0]):
        table = table + jnp.where(expert == routes[k : k + 1, :], gain[k : k + 1, :], 0.0)
    gtab[...] = table
    for k in range(1, 2 * NZ):
        gain_copy(k).start()

    rows[pl.ds(pl.multiple_of((c * NZ + z) * n_tok, n_tok), n_tok), :] = tok[...]
    gains[c * NZ + z] = gtab[...]

    def hop(h):
        left, right = z - 1 - h, z + 1 + h

        @pl.when(left >= 0)
        def _():
            tok_wait(left, c)

            @pl.when(has_next)
            def _():
                tok_copy(block(left, c), left, tok_sr, nxt).start()

            tok_copy(block(left, c), left, tok_ss, sib).start()

        @pl.when(right <= NZ - 1)
        def _():
            tok_wait(right, c)

            @pl.when(has_prev)
            def _():
                tok_copy(block(right, c), right, tok_sl, prv).start()

            tok_copy(block(right, c), right, tok_ss, sib).start()

    def pass_on(i):
        own_x(i).wait_recv()
        relay_y(i).start()
        own_y(i).wait_recv()
        relay_x(i).start()

    tile = 2 * n_tok
    tiles = rows.shape[0] // tile
    half_line = NZ // 2
    mine = z // half_line

    def partial_tile(acc, w, owner, first, i):
        at = pl.ds(pl.multiple_of(owner * depth, depth), depth)
        r = pl.ds(pl.multiple_of(i * tile, tile), tile)
        p = jnp.dot(rows[r, at], w[...], preferred_element_type=jnp.float32)
        acc[r, :] = p if first else acc[r, :] + p

    def own_tiles(line_half):
        def body(cc, carry):
            i = cc * half_line + line_half
            partial_tile(acc_g, gw, g, True, i)
            partial_tile(acc_u, uw, g, True, i)
            return carry

        lax.fori_loop(0, 2, body, 0)

    hop(0)
    fetch(0).wait()
    fetch(1).wait()
    for k in range(half_line):
        tok_wait(mine * half_line + k, 1 - c)
    own_tiles(mine)
    hop(1)
    pass_on(0)
    hop(2)
    pass_on(1)

    for k in range(1, 2 * NZ):
        peer = (ep + k) % (2 * NZ)
        at = (peer % 2) * NZ + peer // 2
        remote(gtab, gains.at[at], gain_s.at[0], gain_r.at[at], sib).wait_recv()
    for b in range(2 * NZ):
        table = gains[b]
        chosen = lax.broadcasted_iota(jnp.int32, table.shape, 0) == ep
        line = jnp.sum(jnp.where(chosen, table, 0.0), axis=0, keepdims=True)
        scale[b * n_tok : (b + 1) * n_tok, :] = jnp.broadcast_to(line, (n_tok, n_tok)).T
    for k in range(half_line):
        tok_wait((1 - mine) * half_line + k, 1 - c)

    def partial(acc, w, owner, first):
        def body(i, carry):
            partial_tile(acc, w, owner, first, i)
            return carry

        lax.fori_loop(0, tiles, body, 0)

    own_tiles(1 - mine)
    partial(acc_g, gin.at[0], gx, False)
    partial(acc_g, gin.at[1], gy, False)
    partial(acc_u, uin.at[0], gx, False)
    partial(acc_u, uin.at[1], gy, False)
    relay_y(0).wait_recv()
    relay_x(0).wait_recv()
    own_x(2).start()
    own_y(2).start()
    partial(acc_g, gin.at[2], gd, False)
    relay_y(1).wait_recv()
    relay_x(1).wait_recv()
    partial(acc_u, uin.at[2], gd, False)

    def act(i, carry):
        r = pl.ds(pl.multiple_of(i * n_tok, n_tok), n_tok)
        gate = acc_g[r, :]
        hid[r, :] = (gate / (1.0 + jnp.exp(-gate)) * acc_u[r, :]).astype(hid.dtype)
        return carry

    lax.fori_loop(0, rows.shape[0] // n_tok, act, 0)

    def sib_copy(q):
        return remote(sout.at[q], sin.at[q], sib_s.at[q], sib_r.at[q], sib)

    def answers(q, w):
        per = tile // n_tok

        def weighted(cc, i):
            at = pl.multiple_of(cc * NZ * n_tok + i * tile, tile)
            p = jnp.dot(hid[pl.ds(at, tile), :], w[...], preferred_element_type=jnp.float32)
            s = scale[pl.ds(at, tile), :]
            p = p * jnp.concatenate([s] * (cols // n_tok), axis=1)
            return p.reshape(per, n_tok, cols)

        def away(i, carry):
            sout[q, pl.ds(i * per, per)] = weighted(1 - c, i).astype(sout.dtype)
            return carry

        def here(i, carry):
            part[q, pl.ds(i * per, per)] = weighted(c, i)
            return carry

        lax.fori_loop(0, NZ // per, away, 0)
        sib_copy(q).start()
        lax.fori_loop(0, NZ // per, here, 0)
        sib_copy(q).wait_recv()

    def right_copy(q, d):
        return remote(rout.at[q, d], rin.at[q, d], right_s.at[q, d], right_r.at[q, d], nxt)

    def left_copy(q, d):
        return remote(rout.at[q, d], lin.at[q, d], left_s.at[q, d], left_r.at[q, d], prv)

    def ends(q):
        @pl.when(z == 0)
        def _():
            for d in range(NZ - 1, 0, -1):
                rout[q, d] = (part[q, d] + sin[q, d].astype(jnp.float32)).astype(rout.dtype)
                right_copy(q, d).start()

        @pl.when(z == NZ - 1)
        def _():
            for d in range(NZ - 1):
                rout[q, d] = (part[q, d] + sin[q, d].astype(jnp.float32)).astype(rout.dtype)
                left_copy(q, d).start()

    def go_right(q, d):
        right_copy(q, d).wait_recv()
        rout[q, d] = (
            part[q, d] + sin[q, d].astype(jnp.float32) + rin[q, d].astype(jnp.float32)
        ).astype(rout.dtype)
        right_copy(q, d).start()

    def go_left(q, d):
        left_copy(q, d).wait_recv()
        rout[q, d] = (
            part[q, d] + sin[q, d].astype(jnp.float32) + lin[q, d].astype(jnp.float32)
        ).astype(rout.dtype)
        left_copy(q, d).start()

    def near(q):
        @pl.when(z == 1)
        def _():
            for d in range(NZ - 1, 1, -1):
                go_right(q, d)

        @pl.when(z == NZ - 2)
        def _():
            for d in range(NZ - 2):
                go_left(q, d)

    def far(q):
        @pl.when(z == NZ - 2)
        def _():
            go_right(q, NZ - 1)

        @pl.when(z == 1)
        def _():
            go_left(q, 0)

    def finish(q, owner):
        at = pl.ds(pl.multiple_of(owner * cols, cols), cols)
        total[:, at] = tok[:, at].astype(jnp.float32) + part[q, z] + sin[q, z].astype(jnp.float32)

        @pl.when(has_prev)
        def _():
            right_copy(q, z).wait_recv()
            total[:, at] = total[:, at] + rin[q, z].astype(jnp.float32)

        @pl.when(has_next)
        def _():
            left_copy(q, z).wait_recv()
            total[:, at] = total[:, at] + lin[q, z].astype(jnp.float32)

    q_half = qw.shape[0] // 2
    q_quarter = q_half // 2
    half_at = pl.ds(pl.multiple_of(c * q_half, q_half), q_half)
    first_at = pl.ds(pl.multiple_of(c * q_half, q_quarter), q_quarter)
    second_at = pl.ds(pl.multiple_of(c * q_half + q_quarter, q_quarter), q_quarter)

    def q_copy(k):
        if k == 0:
            return remote(qw_far.at[half_at], qin.at[0, half_at], q_s.at[0], q_r.at[0], x_dev)
        if k == 1:
            return remote(qw_far.at[half_at], qin.at[1, half_at], q_s.at[1], q_r.at[1], y_dev)
        if k == 2:
            return remote(qin.at[0, first_at], qin.at[2, first_at], q_s.at[2], q_r.at[2], y_dev)
        if k == 3:
            return remote(qin.at[1, second_at], qin.at[2, second_at], q_s.at[3], q_r.at[3], x_dev)
        slot, at = ((0, half_at), (1, half_at), (2, first_at), (2, second_at))[k - 4]
        return remote(qin.at[slot, at], qin.at[slot, at], q_s.at[k], q_r.at[k], sib)

    other_half = pl.ds(pl.multiple_of((1 - c) * q_half, q_half), q_half)
    other_first = pl.ds(pl.multiple_of((1 - c) * q_half, q_quarter), q_quarter)
    other_second = pl.ds(pl.multiple_of((1 - c) * q_half + q_quarter, q_quarter), q_quarter)

    def q_wait_sib(k):
        slot, at = ((0, other_half), (1, other_half), (2, other_first), (2, other_second))[k - 4]
        remote(qin.at[slot, at], qin.at[slot, at], q_s.at[k], q_r.at[k], sib).wait_recv()

    fetch(2).wait()
    answers(0, dw)
    ends(0)
    pass_on(2)
    near(0)
    answers(1, din.at[0])
    ends(1)
    far(0)
    answers(2, din.at[1])
    ends(2)
    near(1)
    relay_y(2).wait_recv()
    relay_x(2).wait_recv()
    q_copy(0).start()
    q_copy(1).start()
    answers(3, din.at[2])
    ends(3)
    far(1)
    near(2)
    far(2)
    near(3)
    finish(0, g)
    finish(1, gx)
    q_copy(0).wait_recv()
    q_copy(2).start()
    q_copy(4).start()
    q_copy(1).wait_recv()
    q_copy(3).start()
    q_copy(5).start()
    far(3)
    finish(2, gy)
    finish(3, gd)

    value = total[...]
    mixed[...] = value.astype(mixed.dtype)
    square = jnp.sum(value * value, axis=-1, keepdims=True) * (1.0 / width)
    normed[...] = (value * lax.rsqrt(square + 1e-06) * ng[...]).astype(normed.dtype)

    def project(w, owner):
        at = pl.ds(pl.multiple_of(owner * qcols, qcols), qcols)
        query[:, at] = jnp.dot(
            normed[...], w[...], preferred_element_type=jnp.float32
        ).astype(query.dtype)

    fetch(3).wait()
    project(qw, g)
    q_wait_sib(4)
    project(qin.at[0], gx)
    q_wait_sib(5)
    project(qin.at[1], gy)
    q_copy(2).wait_recv()
    q_copy(6).start()
    q_copy(3).wait_recv()
    q_copy(7).start()
    q_wait_sib(6)
    q_wait_sib(7)
    project(qin.at[2], gd)

    for k in range(1, 2 * NZ):
        gain_copy(k).wait_send()
    for zz in range(NZ):
        @pl.when(has_next & (zz <= z))
        def _():
            tok_copy(tok, zz, tok_sr, nxt).wait_send()

        @pl.when(has_prev & (zz >= z))
        def _():
            tok_copy(tok, zz, tok_sl, prv).wait_send()

        tok_copy(tok, zz, tok_ss, sib).wait_send()
    for i in range(3):
        for copy in (own_x, own_y, relay_x, relay_y):
            copy(i).wait_send()
    for k in range(8):
        q_copy(k).wait_send()
    for q in range(4):
        sib_copy(q).wait_send()
        for d in range(NZ):
            if d > 0:
                @pl.when(z < d)
                def _():
                    right_copy(q, d).wait_send()
            if d < NZ - 1:
                @pl.when(z > d)
                def _():
                    left_copy(q, d).wait_send()


def fused(tokens, routes, route_gain, gate_weight, up_weight, down_weight, norm_gain, query_weight):
    n_tok, width = tokens.shape
    hidden = gate_weight.shape[2]
    depth, cols, qcols = gate_weight.shape[1], down_weight.shape[2], query_weight.shape[1]
    n_rows = 2 * NZ * n_tok
    vmem = pl.BlockSpec(memory_space=pltpu.VMEM)
    hbm = pl.BlockSpec(memory_space=pl.ANY)
    b16, f32 = jnp.bfloat16, jnp.float32
    dma = pltpu.SemaphoreType.DMA
    return pl.pallas_call(
        kernel,
        out_shape=(
            jax.ShapeDtypeStruct((n_tok, width), b16),
            jax.ShapeDtypeStruct((n_tok, 4 * qcols), b16),
        ),
        in_specs=[vmem] * 3 + [hbm] * 3 + [vmem, hbm],
        out_specs=(vmem, vmem),
        scratch_shapes=[
            pltpu.VMEM((depth, hidden), b16),
            pltpu.VMEM((depth, hidden), b16),
            pltpu.VMEM((hidden, cols), b16),
            pltpu.VMEM((width, qcols), b16),
            pltpu.VMEM((n_rows, width), b16),
            pltpu.VMEM((2 * NZ, n_tok), f32),
            pltpu.VMEM((2 * NZ, 2 * NZ, n_tok), f32),
            pltpu.VMEM((n_rows, n_tok), f32),
            pltpu.VMEM((3, depth, hidden), b16),
            pltpu.VMEM((3, depth, hidden), b16),
            pltpu.VMEM((3, hidden, cols), b16),
            pltpu.VMEM((3, width, qcols), b16),
            pltpu.VMEM((n_rows, hidden), f32),
            pltpu.VMEM((n_rows, hidden), f32),
            pltpu.VMEM((n_rows, hidden), b16),
            pltpu.VMEM((4, NZ, n_tok, cols), b16),
            pltpu.VMEM((4, NZ, n_tok, cols), b16),
            pltpu.VMEM((4, NZ, n_tok, cols), f32),
            pltpu.VMEM((4, NZ, n_tok, cols), b16),
            pltpu.VMEM((4, NZ, n_tok, cols), b16),
            pltpu.VMEM((4, NZ, n_tok, cols), b16),
            pltpu.VMEM((n_tok, width), f32),
            pltpu.VMEM((n_tok, width), b16),
            dma((2 * NZ,)),
            dma((2 * NZ,)),
            dma((2 * NZ,)),
            dma((NZ,)),
            dma((NZ,)),
            dma((NZ,)),
            dma((3, 4)),
            dma((3, 4)),
            dma((8,)),
            dma((8,)),
            dma((4,)),
            dma((4,)),
            dma((4, NZ)),
            dma((4, NZ)),
            dma((4, NZ)),
            dma((4, NZ)),
            dma((4,)),
        ],
        compiler_params=pltpu.CompilerParams(
            collective_id=0, has_side_effects=True, vmem_limit_bytes=60 * 1024 * 1024
        ),
    )(
        tokens, routes.T, route_gain.T, gate_weight[0], up_weight[0], down_weight[0],
        norm_gain.reshape(1, width), query_weight,
    )


def general(
    tokens, routes, route_gain, gate_weight, up_weight, down_weight, norm_gain, query_weight
):
    ep_count = lax.axis_size("ep")
    tok_rows = tokens.shape[0]
    width = tokens.shape[1]
    choose = routes.shape[1]
    capacity = 8 * tok_rows // ep_count
    flat = routes.reshape(-1)
    onehot = (flat[:, None] == jnp.arange(ep_count, dtype=jnp.int32)[None, :]).astype(jnp.int32)
    counted = jnp.cumsum(onehot, axis=0)
    rank = jnp.sum(onehot * (counted - 1), axis=1)
    slot = flat * capacity + rank
    repeated = jnp.repeat(tokens, choose, axis=0)
    outbound = jnp.zeros((ep_count * capacity, width), jnp.bfloat16).at[slot].set(repeated)
    arrived = lax.all_to_all(outbound, "ep", split_axis=0, concat_axis=0, tiled=True)
    gate = jnp.dot(
        arrived,
        lax.all_gather(gate_weight[0], "grp", axis=0, tiled=True),
        preferred_element_type=jnp.float32,
    )
    up = jnp.dot(
        arrived,
        lax.all_gather(up_weight[0], "grp", axis=0, tiled=True),
        preferred_element_type=jnp.float32,
    )
    hidden = (jax.nn.silu(gate) * up).astype(jnp.bfloat16)
    answers = jnp.dot(
        hidden,
        lax.all_gather(down_weight[0], "grp", axis=1, tiled=True),
        preferred_element_type=jnp.float32,
    ).astype(jnp.bfloat16)
    returned = lax.all_to_all(answers, "ep", split_axis=0, concat_axis=0, tiled=True)
    picked = returned[slot].reshape(tok_rows, choose, width).astype(jnp.float32)
    total = tokens.astype(jnp.float32) + jnp.sum(picked * route_gain[:, :, None], axis=1)
    square = jnp.mean(total * total, axis=-1, keepdims=True)
    normed = (total * lax.rsqrt(square + 1e-06) * norm_gain).astype(jnp.bfloat16)
    query = jnp.dot(
        normed,
        lax.all_gather(query_weight, "grp", axis=1, tiled=True),
        preferred_element_type=jnp.float32,
    ).astype(jnp.bfloat16)
    return (total.astype(jnp.bfloat16), query)


def solution(mesh):
    placed = (
        P(("grp", "ep"), None),
        P(("grp", "ep"), None),
        P(("grp", "ep"), None),
        P("ep", "grp", None),
        P("ep", "grp", None),
        P("ep", None, "grp"),
        P(),
        P(None, "grp"),
    )
    small = mesh.shape["grp"] == 4 and mesh.shape["ep"] == 2 * NZ
    return jax.shard_map(
        fused if small else general,
        mesh=mesh,
        in_specs=placed,
        out_specs=(P(("grp", "ep"), None), P(("grp", "ep"), None)),
        check_vma=False,
    )
```
